1024 devices in a mesh: row: 64 (over z, core), col: 16 (over x, y).
Axes of the slice: x: 4, y: 4, z: 32, core: 2. Of those that a mesh axis runs over, the one named last changes fastest.
Arguments:
- block_values: float32 [16384, 8192], P('col', 'row'), may hold values from -4 to 4
- block_cols: int32 [128, 64], P('col', 'row'), may hold values from 0 to 1, as said below
- section_cols: int32 [2], replicated, may hold values from 0 to 63
Outputs:
- updated: bfloat16 [16384, 8192], P('col', 'row')
The draws below stay inside these ranges and needn't reach their ends.
Inputs may be any that keep to these rules, and one draw needn't show every extreme that they name: `block_cols`: within each block row, the 1 entries belonging to one index of row are distinct.
All inputs are finite; a program needn't handle non-finite values.
Results may differ from the reference program's by a relative error of at most 0.001.
Values sent between devices are 32-bit elements; how exact they have to be, the bound alone decides.
A program may use at most 32 MiB of HBM per device.

```python
import jax
import jax.numpy as jnp
from jax import lax

BLK = 128
CB = 2
OCC = 1
SECTIONS = 2
NB = 128
N_ROW = 64


def draw_block_cols(key, part):
    key = jax.random.fold_in(key, 7)
    scores = jax.random.randint(key, (NB, N_ROW, CB), 0, 1 << 20, dtype=jnp.int32)
    scores = scores * CB + jnp.arange(CB, dtype=jnp.int32)
    chosen = jnp.argsort(scores, axis=-1, stable=True)[:, :, :OCC]
    return chosen.astype(jnp.int32).reshape(NB, N_ROW * OCC)


def block_levels(own_key, dims, cuts, low, high):
    def one(dim, parts):
        steps = jax.random.uniform(jax.random.fold_in(jax.random.fold_in(own_key, 6), dim), (parts,), jnp.float32, low / len(cuts), high / len(cuts))
        return jnp.repeat(jnp.exp(steps), dims[dim] // parts).reshape((-1,) + (1,) * (len(dims) - dim - 1))

    level = one(*cuts[0])
    for cut in cuts[1:]:
        level = level * one(*cut)
    return level


def gaussian(stream_key, shape, scale, limit, split=(), held_as=jnp.bfloat16):
    entries = scale * jax.random.normal(stream_key, shape, jnp.float32)
    if split:
        entries = entries * block_levels(stream_key, shape, split, -0.22, 0.18)
    return jnp.clip(entries, -limit, limit).astype(held_as)


def setup_inputs(seed: int = 0) -> dict:
    key_list = jax.random.split(jax.random.key(seed), 4)
    block_values = gaussian(key_list[0], (NB * BLK, N_ROW * OCC * BLK), (BLK ** -0.25), 4.0, ((0, 16), (1, 64)), jnp.float32)
    block_cols = draw_block_cols(jax.random.fold_in(key_list[3], 71), 0)
    section_cols = jax.random.randint(key_list[2], (SECTIONS,), 0, N_ROW).astype(jnp.int32)
    return {"block_values": block_values, "block_cols": block_cols, "section_cols": section_cols}


def contribution(panel_values, source_rows, own_values, own_cols):
    picked = own_values[source_rows]
    picked_cols = own_cols[source_rows]
    matches = (picked_cols[:, :, None, :] == own_cols[:, None, :, None]).astype(jnp.float32)
    selected = jnp.einsum("ipgq,ipyqz->ipgyz", matches, picked, precision=lax.Precision.HIGHEST)
    return jnp.einsum("ixpy,ipgyz->ixgz", panel_values, selected, precision=lax.Precision.HIGHEST)


def reference(block_values, block_cols, section_cols):
    grouped = block_values.reshape(NB, BLK, N_ROW, OCC, BLK)
    grouped_cols = block_cols.reshape(NB, N_ROW, OCC)

    def column(group):
        own_values = lax.dynamic_index_in_dim(grouped, group, 2, keepdims=False)
        own_cols = lax.dynamic_index_in_dim(grouped_cols, group, 1, keepdims=False)
        total = jnp.zeros((NB, BLK, OCC, BLK), jnp.float32)
        for section_index in range(SECTIONS):
            first_group = section_cols[section_index]
            panel_values = lax.dynamic_index_in_dim(grouped, first_group, 2, keepdims=False)
            panel_cols = lax.dynamic_index_in_dim(grouped_cols, first_group, 1, keepdims=False)
            source_rows = (first_group * CB + panel_cols).astype(jnp.int32)
            total = total + contribution(panel_values, source_rows, own_values, own_cols)
        updated = 1.5 * own_values - 0.5 * total - 0.1 * total * total * total
        return updated.astype(jnp.bfloat16).reshape(NB * BLK, OCC * BLK)

    stacked = lax.map(column, jnp.arange(N_ROW, dtype=jnp.int32))
    return jnp.transpose(stacked, (1, 0, 2)).reshape(NB * BLK, N_ROW * OCC * BLK)
```

```python
import functools

import jax
import jax.numpy as jnp
from jax import lax
from jax.experimental import pallas as pl
from jax.experimental.pallas import tpu as pltpu
from jax.sharding import PartitionSpec as P

MESH = pl.DeviceIdType.MESH
BLK = 128
TILE = 8
UNITS = 8
STRIDE = 4
GROUPS = 3
PER = 3
CHUNKS = GROUPS * PER
LANES = 5
SIDE = 4


def broadcast_multiply(
    n_row, sec_ref, cols_ref, x_hbm, o_ref,
    xv, xs, raw, rawh, cand, tx, rx, pan, sib, stage, bx, by, bnd, wh, wl,
    x_sem, rs_s, rs_r, rh_s, rh_r, cv_s, cv_r, ag_s, ag_r, ah_s, ah_r, sb_s, sb_r, bs_s, bs_r,
):
    chips = n_row // 2
    blocks = chips // STRIDE
    hops = (blocks // 2, (blocks - 1) // 2)
    slots = tuple(CHUNKS + LANES * (d - 1) for d in hops)
    row = lax.axis_index("row")
    col = lax.axis_index("col")
    z, core = lax.div(row, 2), lax.rem(row, 2)
    cx, cy = lax.div(col, SIDE), lax.rem(col, SIDE)

    def at(dz, k):
        return lax.rem(z + dz + chips, chips) * 2 + k

    def unit(r):
        return lax.rem(r, UNITS)

    sibling = at(0, 1 - core)
    near = [at(dz, k) for dz in (-1, 1) for k in (0, 1)]
    far = [at(dz, k) for dz in (-2, 2) for k in (0, 1)]
    xs_peers = [lax.rem(cx + d, SIDE) for d in range(1, SIDE)]
    ys_peers = [lax.rem(cy + d, SIDE) for d in range(1, SIDE)]

    barrier = pltpu.get_barrier_semaphore()
    greet = [(r, col) for r in near + far + [sibling]]
    greet += [(row, px * SIDE + cy) for px in xs_peers]
    greet += [(row, cx * SIDE + py) for py in ys_peers]
    for device in greet:
        pl.semaphore_signal(barrier, inc=1, device_id=device, device_id_type=MESH)

    load = pltpu.make_async_copy(x_hbm, xv, x_sem)
    load.start()
    load.wait()

    sent = []

    def send(src, dst, send_sem, recv_sem, device):
        copy = pltpu.make_async_remote_copy(
            src_ref=src, dst_ref=dst, send_sem=send_sem, recv_sem=recv_sem,
            device_id=device, device_id_type=MESH,
        )
        copy.start()
        sent.append(copy)
        return copy

    for u in range(UNITS):
        mark = jnp.full((TILE, BLK), cols_ref[u, 0].astype(jnp.float32), jnp.float32)
        for h in range(2):
            xs[u, 0, h, 0] = mark
            for k in range(1, CHUNKS):
                first = u * BLK + h * (BLK // 2) + (k - 1) * TILE
                xs[u, k // PER, h, k % PER] = xv[first : first + TILE, :]
    groups = [jnp.full((TILE, BLK), sec_ref[s], jnp.int32) for s in range(2)]
    for s in range(2):
        for q in range(2):
            for first in range(0, BLK + TILE, TILE):
                value = None
                for i in range(UNITS // 2):
                    u = 2 * i + q
                    if first == 0:
                        piece = jnp.full((TILE, BLK), cols_ref[u, 0].astype(jnp.float32), jnp.float32)
                    else:
                        start = u * BLK + first - TILE
                        piece = xv[start : start + TILE, :]
                    value = piece if i == 0 else jnp.where((groups[s] & 3) == i, piece, value)
                stage[2 * s + q, first : first + TILE] = value

    pl.semaphore_wait(barrier, len(greet))

    full_copies, half_copies = [], []
    for g in range(GROUPS):
        line = []
        for dz in (1, -1):
            for k in (0, 1):
                r = at(dz, k)
                slot = (1 if dz == 1 else 3) + core
                i = (0 if dz == 1 else 2) + k
                line.append(send(
                    xs.at[unit(r), g], raw.at[slot, g], rs_s.at[i, g], rs_r.at[slot, g], (r, col)
                ))
        line.append(send(
            xs.at[unit(sibling), g], raw.at[0, g], rs_s.at[4, g], rs_r.at[0, g], (sibling, col)
        ))
        full_copies.append(line)
        for dz in (2, -2):
            for k in (0, 1):
                r = at(dz, k)
                h = 0 if dz == 2 else 1
                slot = 2 * h + core
                i = 2 * h + k
                half_copies.append(send(
                    xs.at[unit(r), g, h], rawh.at[slot, g], rh_s.at[i, g], rh_r.at[slot, g], (r, col)
                ))

    def spread(src, dst, mine, peers, device, step):
        for d, p in enumerate(peers):
            send(src(p), dst.at[mine], bs_s.at[step, d], bs_r.at[step, mine], device(p))

    def arrived(dst, peers, step):
        for p in peers:
            pltpu.make_async_copy(dst.at[p], dst.at[p], bs_r.at[step, p]).wait()

    spread(lambda p: stage.at[p], bx, cx, xs_peers, lambda p: (row, p * SIDE + cy), 0)

    where_right = []
    for h in range(2):
        line = []
        for s in range(2):
            e = (z - (groups[s] >> 1)) & (chips - 1)
            m = e & (STRIDE - 1)
            v = jnp.where(m == 2, 2 if h == 0 else -2, jnp.where(m == 3, -1, m))
            line.append(((e - v) & (chips - 1)) >> 2)
        where_right.append(line)

    def wait_for(dst, sem):
        pltpu.make_async_copy(dst, dst, sem).wait()

    me_unit = unit(row)
    sources = [sibling] + near
    right4 = (at(STRIDE, core), col)
    left4 = (at(-STRIDE, core), col)

    def candidate(k):
        g, c = k // PER, k % PER
        for h in range(2):
            own = xs[me_unit, g, h, c]
            pieces = [(sources[i], raw[i, g, h, c]) for i in range(5)]
            pieces += [(far[2 * h + i], rawh[2 * h + i, g, c]) for i in range(2)]
            for s in range(2):
                value = own
                for r, piece in pieces:
                    value = jnp.where(groups[s] == r, piece, value)
                cand[k, h, s] = value
                pan[0, g, h, s, c] = value

    def consume(d, t):
        for hop in range(1, hops[d] + 1):
            k = t - LANES * (hop - 1)
            if 0 <= k < CHUNKS:
                g, c = k // PER, k % PER
                place = hop if d == 0 else blocks - hop
                for h in range(2):
                    for s in range(2):
                        pan[0, g, h, s, c] = jnp.where(
                            where_right[h][s] == place, rx[d, t, h, s], pan[0, g, h, s, c]
                        )

    def gather(g):
        send(pan.at[0, g], pan.at[1, g], ag_s.at[0, g], ag_r.at[0, g], (at(1, core), col))
        send(pan.at[0, g], pan.at[2, g], ag_s.at[1, g], ag_r.at[1, g], (at(-1, core), col))
        send(pan.at[0, g, 0], pan.at[3, g, 0], ah_s.at[0, g], ah_r.at[0, g], (at(2, core), col))
        send(pan.at[0, g, 1], pan.at[3, g, 1], ah_s.at[1, g], ah_r.at[1, g], (at(-2, core), col))
        send(pan.at[0, g], sib.at[0, g], sb_s.at[0, g], sb_r.at[0, g], (sibling, col))

    def pick(dst, into, mine, own, peers, place):
        for first in range(0, BLK + TILE, TILE):
            rows = pl.ds(first, TILE)
            value = own(rows)
            for p in peers:
                value = jnp.where(place == p, dst[p, rows], value)
            into[mine, rows] = value

    my_group = jnp.full((TILE, BLK), sec_ref[lax.div(cx, 2)], jnp.int32)

    def band_step_two():
        arrived(bx, xs_peers, 0)
        pick(bx, by, cy, lambda rows: stage[cx, rows], xs_peers, my_group >> 4)
        spread(lambda p: by.at[cy], by, cy, ys_peers, lambda p: (row, cx * SIDE + p), 1)

    def band_step_three():
        arrived(by, ys_peers, 1)
        pick(by, bnd, cx, lambda rows: by[cy, rows], ys_peers, (my_group >> 2) & 3)
        spread(lambda p: bnd.at[cx], bnd, cx, xs_peers, lambda p: (row, p * SIDE + cy), 2)

    def band_ready():
        arrived(bnd, xs_peers, 2)
        for s in range(2):
            for q in range(2):
                value = bnd[2 * s + q, TILE:]
                high = value.astype(jnp.bfloat16)
                low = (value - high.astype(jnp.float32)).astype(jnp.bfloat16)
                wh[s, :BLK, q * BLK : (q + 1) * BLK] = high
                wh[s, BLK:, q * BLK : (q + 1) * BLK] = high
                wl[s, :, q * BLK : (q + 1) * BLK] = low

    def received(d, t):
        wait_for(rx.at[d, t], cv_r.at[d, t])

    def finish(t):
        k = t - LANES * (hops[0] - 1)
        if k >= 0 and k % PER == PER - 1:
            gather(k // PER)

    for t in range(slots[0]):
        if t < CHUNKS and t % PER == 0:
            g = t // PER
            for i in range(5):
                wait_for(raw.at[i, g], rs_r.at[i, g])
            for i in range(4):
                wait_for(rawh.at[i, g], rh_r.at[i, g])
            for k in range(t, t + PER):
                candidate(k)
        for d in range(2):
            if t >= slots[d]:
                continue
            target = right4 if d == 0 else left4
            if t >= LANES:
                received(d, t - LANES)
            if t < CHUNKS:
                for h in range(2):
                    for s in range(2):
                        value = cand[t, h, s]
                        if t >= LANES:
                            value = jnp.where(where_right[h][s] == 0, value, rx[d, t - LANES, h, s])
                        tx[d, t, h, s] = value
                source = tx.at[d, t]
            else:
                source = rx.at[d, t - LANES]
            send(source, rx.at[d, t], cv_s.at[d, t], cv_r.at[d, t], target)
        if t >= LANES:
            for d in range(2):
                if t < slots[d]:
                    consume(d, t - LANES)
            if t >= slots[1] and t - LANES < slots[1]:
                received(1, t - LANES)
                consume(1, t - LANES)
            finish(t - LANES)
        if t == LANES - 1:
            band_step_two()
        if t == 2 * LANES - 1:
            band_step_three()
        if t == 3 * LANES - 1:
            band_ready()
    for t in range(slots[0] - LANES, slots[0]):
        if t < slots[1]:
            received(1, t)
            consume(1, t)
        received(0, t)
        consume(0, t)
        finish(t)

    def multiply(buf, i, u):
        total = jnp.zeros((BLK, BLK), jnp.float32)
        own_col = cols_ref[u, 0].astype(jnp.float32)
        for s in range(2):
            tiles = [
                buf[i, k // PER, h, s, k % PER] for h in range(2) for k in range(1, CHUNKS)
            ]
            value = jnp.concatenate(tiles, axis=0)
            high = value.astype(jnp.bfloat16)
            low = (value - high.astype(jnp.float32)).astype(jnp.bfloat16)
            both = jnp.concatenate([high, low], axis=1)
            product = jnp.dot(both, wh[s], preferred_element_type=jnp.float32)
            product += jnp.dot(high, wl[s], preferred_element_type=jnp.float32)
            second = buf[i, 0, 0, s, 0][0:1, :] > 0.5
            mark = jnp.where(second, bnd[2 * s + 1, 0:1, :], bnd[2 * s, 0:1, :])
            part = jnp.where(second, product[:, BLK:], product[:, :BLK])
            total += jnp.where(mark == own_col, part, 0.0)
        rows = pl.ds(pl.multiple_of(u * BLK, BLK), BLK)
        own = xv[rows, :]
        o_ref[rows, :] = (1.5 * own - 0.5 * total - 0.1 * total * total * total).astype(jnp.bfloat16)

    steps = (0, -2, 2, 4)

    def unit_at(r, i):
        return lax.rem(r + steps[i] + UNITS, UNITS)

    for i in (1, 2, 3):
        for g in range(GROUPS):
            if i < 3:
                wait_for(pan.at[i, g], ag_r.at[i - 1, g])
            else:
                wait_for(pan.at[3, g, 0], ah_r.at[0, g])
                wait_for(pan.at[3, g, 1], ah_r.at[1, g])
            send(pan.at[i, g], sib.at[i, g], sb_s.at[i, g], sb_r.at[i, g], (sibling, col))
    for i in range(4):
        multiply(pan, i, unit_at(row, i))
    for i in range(4):
        for g in range(GROUPS):
            wait_for(sib.at[i, g], sb_r.at[i, g])
        multiply(sib, i, unit_at(sibling, i))
    for copy in sent:
        copy.wait_send()


def shards(n_row, block_values, block_cols, section_cols):
    blocks = n_row // 2 // STRIDE
    slots = CHUNKS + LANES * (blocks // 2 - 1)
    f32 = jnp.float32
    part = (2, PER, TILE, BLK)
    packet = (2, 2, TILE, BLK)
    held = (GROUPS, 2, 2, PER, TILE, BLK)
    band = (TILE + BLK, BLK)
    dma = pltpu.SemaphoreType.DMA
    return pl.pallas_call(
        functools.partial(broadcast_multiply, n_row),
        out_shape=jax.ShapeDtypeStruct(block_values.shape, jnp.bfloat16),
        in_specs=[
            pl.BlockSpec(memory_space=pltpu.SMEM),
            pl.BlockSpec(memory_space=pltpu.SMEM),
            pl.BlockSpec(memory_space=pl.ANY),
        ],
        out_specs=pl.BlockSpec(memory_space=pltpu.VMEM),
        scratch_shapes=[
            pltpu.VMEM(block_values.shape, f32),
            pltpu.VMEM((UNITS, GROUPS) + part, f32),
            pltpu.VMEM((5, GROUPS) + part, f32),
            pltpu.VMEM((4, GROUPS) + part[1:], f32),
            pltpu.VMEM((CHUNKS,) + packet, f32),
            pltpu.VMEM((2, CHUNKS) + packet, f32),
            pltpu.VMEM((2, slots) + packet, f32),
            pltpu.VMEM((4,) + held, f32),
            pltpu.VMEM((4,) + held, f32),
            pltpu.VMEM((4,) + band, f32),
            pltpu.VMEM((4,) + band, f32),
            pltpu.VMEM((4,) + band, f32),
            pltpu.VMEM((4,) + band, f32),
            pltpu.VMEM((2, 2 * BLK, 2 * BLK), jnp.bfloat16),
            pltpu.VMEM((2, BLK, 2 * BLK), jnp.bfloat16),
            dma,
            dma((5, GROUPS)), dma((5, GROUPS)),
            dma((4, GROUPS)), dma((4, GROUPS)),
            dma((2, slots)), dma((2, slots)),
            dma((2, GROUPS)), dma((2, GROUPS)),
            dma((2, GROUPS)), dma((2, GROUPS)),
            dma((4, GROUPS)), dma((4, GROUPS)),
            dma((3, SIDE - 1)), dma((3, SIDE)),
        ],
        compiler_params=pltpu.CompilerParams(
            collective_id=0, has_side_effects=True, vmem_limit_bytes=32 * 1024 * 1024
        ),
        cost_estimate=pl.CostEstimate(flops=400_000_000, bytes_accessed=800_000, transcendentals=0),
        name="broadcast_multiply",
    )(section_cols, block_cols, block_values)


def solution(mesh):
    return jax.shard_map(
        functools.partial(shards, mesh.shape["row"]),
        mesh=mesh,
        in_specs=(P("col", "row"), P("col", "row"), P()),
        out_specs=P("col", "row"),
        check_vma=False,
    )
```

```python
import functools

import jax
import jax.numpy as jnp
from jax import lax
from jax.experimental import pallas as pl
from jax.experimental.pallas import tpu as pltpu
from jax.sharding import PartitionSpec as P

MESH = pl.DeviceIdType.MESH
BLK = 128
TILE = 8
UNITS = 8
STRIDE = 4
GROUPS = 3
PER = 3
CHUNKS = GROUPS * PER
LANES = 4
SIDE = 4


def broadcast_multiply(
    n_row, sec_ref, cols_ref, x_hbm, o_ref,
    xv, xs, raw, rawh, cand, tx, rx, pan, sib, stage, bx, by, bnd, wh, wl,
    x_sem, rs_s, rs_r, rh_s, rh_r, cv_s, cv_r, ag_s, ag_r, ah_s, ah_r, sb_s, sb_r, bs_s, bs_r,
):
    chips = n_row // 2
    blocks = chips // STRIDE
    far_hop = blocks // 2
    slots = CHUNKS + LANES * (far_hop - 1)
    whole = slots - LANES
    row = lax.axis_index("row")
    col = lax.axis_index("col")
    z, core = lax.div(row, 2), lax.rem(row, 2)
    cx, cy = lax.div(col, SIDE), lax.rem(col, SIDE)

    def at(dz, k):
        return lax.rem(z + dz + chips, chips) * 2 + k

    def unit(r):
        return lax.rem(r, UNITS)

    sibling = at(0, 1 - core)
    near = [at(dz, k) for dz in (-1, 1) for k in (0, 1)]
    far = [at(dz, k) for dz in (-2, 2) for k in (0, 1)]
    xs_peers = [lax.rem(cx + d, SIDE) for d in range(1, SIDE)]
    ys_peers = [lax.rem(cy + d, SIDE) for d in range(1, SIDE)]

    barrier = pltpu.get_barrier_semaphore()
    greet = [(r, col) for r in near + far + [sibling]]
    greet += [(row, px * SIDE + cy) for px in xs_peers]
    greet += [(row, cx * SIDE + py) for py in ys_peers]
    for device in greet:
        pl.semaphore_signal(barrier, inc=1, device_id=device, device_id_type=MESH)

    load = pltpu.make_async_copy(x_hbm, xv, x_sem)
    load.start()
    load.wait()

    sent = []

    def send(src, dst, send_sem, recv_sem, device):
        copy = pltpu.make_async_remote_copy(
            src_ref=src, dst_ref=dst, send_sem=send_sem, recv_sem=recv_sem,
            device_id=device, device_id_type=MESH,
        )
        copy.start()
        sent.append(copy)
        return copy

    for u in range(UNITS):
        mark = jnp.full((TILE, BLK), cols_ref[u, 0].astype(jnp.float32), jnp.float32)
        for h in range(2):
            xs[u, 0, h, 0] = mark
            for k in range(1, CHUNKS):
                first = u * BLK + h * (BLK // 2) + (k - 1) * TILE
                xs[u, k // PER, h, k % PER] = xv[first : first + TILE, :]
    groups = [jnp.full((TILE, BLK), sec_ref[s], jnp.int32) for s in range(2)]
    for s in range(2):
        for q in range(2):
            for first in range(0, BLK + TILE, TILE):
                value = None
                for i in range(UNITS // 2):
                    u = 2 * i + q
                    if first == 0:
                        piece = jnp.full((TILE, BLK), cols_ref[u, 0].astype(jnp.float32), jnp.float32)
                    else:
                        start = u * BLK + first - TILE
                        piece = xv[start : start + TILE, :]
                    value = piece if i == 0 else jnp.where((groups[s] & 3) == i, piece, value)
                stage[2 * s + q, first : first + TILE] = value

    pl.semaphore_wait(barrier, len(greet))

    full_copies, half_copies = [], []
    for g in range(GROUPS):
        line = []
        for dz in (1, -1):
            for k in (0, 1):
                r = at(dz, k)
                slot = (1 if dz == 1 else 3) + core
                i = (0 if dz == 1 else 2) + k
                line.append(send(
                    xs.at[unit(r), g], raw.at[slot, g], rs_s.at[i, g], rs_r.at[slot, g], (r, col)
                ))
        line.append(send(
            xs.at[unit(sibling), g], raw.at[0, g], rs_s.at[4, g], rs_r.at[0, g], (sibling, col)
        ))
        full_copies.append(line)
        for dz in (2, -2):
            for k in (0, 1):
                r = at(dz, k)
                h = 0 if dz == 2 else 1
                slot = 2 * h + core
                i = 2 * h + k
                half_copies.append(send(
                    xs.at[unit(r), g, h], rawh.at[slot, g], rh_s.at[i, g], rh_r.at[slot, g], (r, col)
                ))

    def spread(src, dst, mine, peers, device, step):
        for d, p in enumerate(peers):
            send(src(p), dst.at[mine], bs_s.at[step, d], bs_r.at[step, mine], device(p))

    def arrived(dst, peers, step):
        for p in peers:
            pltpu.make_async_copy(dst.at[p], dst.at[p], bs_r.at[step, p]).wait()

    spread(lambda p: stage.at[p], bx, cx, xs_peers, lambda p: (row, p * SIDE + cy), 0)

    where_right = []
    for h in range(2):
        line = []
        for s in range(2):
            e = (z - (groups[s] >> 1)) & (chips - 1)
            m = e & (STRIDE - 1)
            v = jnp.where(m == 2, 2 if h == 0 else -2, jnp.where(m == 3, -1, m))
            line.append(((e - v) & (chips - 1)) >> 2)
        where_right.append(line)

    def wait_for(dst, sem):
        pltpu.make_async_copy(dst, dst, sem).wait()

    me_unit = unit(row)
    sources = [sibling] + near
    right4 = (at(STRIDE, core), col)
    left4 = (at(-STRIDE, core), col)

    def candidate(k):
        g, c = k // PER, k % PER
        for h in range(2):
            own = xs[me_unit, g, h, c]
            pieces = [(sources[i], raw[i, g, h, c]) for i in range(5)]
            pieces += [(far[2 * h + i], rawh[2 * h + i, g, c]) for i in range(2)]
            for s in range(2):
                value = own
                for r, piece in pieces:
                    value = jnp.where(groups[s] == r, piece, value)
                cand[k, h, s] = value
                pan[0, g, h, s, c] = value

    def consume(d, t):
        for hop in range(1, far_hop + 1):
            k = t - LANES * (hop - 1)
            if 0 <= k < CHUNKS:
                g, c = k // PER, k % PER
                place = hop if d == 0 else blocks - hop
                for h in range(2) if hop < far_hop else (d,):
                    for s in range(2):
                        pan[0, g, h, s, c] = jnp.where(
                            where_right[h][s] == place, rx[d, t, h, s], pan[0, g, h, s, c]
                        )

    def gather(g):
        send(pan.at[0, g], pan.at[1, g], ag_s.at[0, g], ag_r.at[0, g], (at(1, core), col))
        send(pan.at[0, g], pan.at[2, g], ag_s.at[1, g], ag_r.at[1, g], (at(-1, core), col))
        send(pan.at[0, g, 0], pan.at[3, g, 0], ah_s.at[0, g], ah_r.at[0, g], (at(2, core), col))
        send(pan.at[0, g, 1], pan.at[3, g, 1], ah_s.at[1, g], ah_r.at[1, g], (at(-2, core), col))
        send(pan.at[0, g], sib.at[0, g], sb_s.at[0, g], sb_r.at[0, g], (sibling, col))

    def pick(dst, into, mine, own, peers, place):
        for first in range(0, BLK + TILE, TILE):
            rows = pl.ds(first, TILE)
            value = own(rows)
            for p in peers:
                value = jnp.where(place == p, dst[p, rows], value)
            into[mine, rows] = value

    my_group = jnp.full((TILE, BLK), sec_ref[lax.div(cx, 2)], jnp.int32)

    def band_step_two():
        arrived(bx, xs_peers, 0)
        pick(bx, by, cy, lambda rows: stage[cx, rows], xs_peers, my_group >> 4)
        spread(lambda p: by.at[cy], by, cy, ys_peers, lambda p: (row, cx * SIDE + p), 1)

    def band_step_three():
        arrived(by, ys_peers, 1)
        pick(by, bnd, cx, lambda rows: by[cy, rows], ys_peers, (my_group >> 2) & 3)
        spread(lambda p: bnd.at[cx], bnd, cx, xs_peers, lambda p: (row, p * SIDE + cy), 2)

    def band_ready():
        arrived(bnd, xs_peers, 2)
        for s in range(2):
            for q in range(2):
                value = bnd[2 * s + q, TILE:]
                high = value.astype(jnp.bfloat16)
                low = (value - high.astype(jnp.float32)).astype(jnp.bfloat16)
                wh[s, :BLK, q * BLK : (q + 1) * BLK] = high
                wh[s, BLK:, q * BLK : (q + 1) * BLK] = high
                wl[s, :, q * BLK : (q + 1) * BLK] = low

    def packet(ref, d, t):
        return ref.at[d, t] if t < whole else ref.at[d, t, d]

    def received(d, t):
        wait_for(packet(rx, d, t), cv_r.at[d, t])

    def finish(t):
        k = t - LANES * (far_hop - 1)
        if k >= 0 and k % PER == PER - 1:
            gather(k // PER)

    for t in range(slots):
        if t < CHUNKS and t % PER == 0:
            g = t // PER
            for i in range(5):
                wait_for(raw.at[i, g], rs_r.at[i, g])
            for i in range(4):
                wait_for(rawh.at[i, g], rh_r.at[i, g])
            for k in range(t, t + PER):
                candidate(k)
        for d in range(2):
            target = right4 if d == 0 else left4
            if t >= LANES:
                received(d, t - LANES)
            if t < CHUNKS:
                for h in range(2):
                    for s in range(2):
                        value = cand[t, h, s]
                        if t >= LANES:
                            value = jnp.where(where_right[h][s] == 0, value, rx[d, t - LANES, h, s])
                        tx[d, t, h, s] = value
                source = tx.at[d, t]
            elif t < whole:
                source = rx.at[d, t - LANES]
            else:
                source = rx.at[d, t - LANES, d]
            send(source, packet(rx, d, t), cv_s.at[d, t], cv_r.at[d, t], target)
        if t >= LANES:
            for d in range(2):
                consume(d, t - LANES)
            finish(t - LANES)
        if t == LANES - 1:
            band_step_two()
        if t == 2 * LANES - 1:
            band_step_three()
        if t == 3 * LANES - 1:
            band_ready()
    for t in range(slots - LANES, slots):
        for d in range(2):
            received(d, t)
            consume(d, t)
        finish(t)

    def multiply(buf, i, u):
        total = jnp.zeros((BLK, BLK), jnp.float32)
        own_col = cols_ref[u, 0].astype(jnp.float32)
        for s in range(2):
            tiles = [
                buf[i, k // PER, h, s, k % PER] for h in range(2) for k in range(1, CHUNKS)
            ]
            value = jnp.concatenate(tiles, axis=0)
            high = value.astype(jnp.bfloat16)
            low = (value - high.astype(jnp.float32)).astype(jnp.bfloat16)
            both = jnp.concatenate([high, low], axis=1)
            product = jnp.dot(both, wh[s], preferred_element_type=jnp.float32)
            product += jnp.dot(high, wl[s], preferred_element_type=jnp.float32)
            second = buf[i, 0, 0, s, 0][0:1, :] > 0.5
            mark = jnp.where(second, bnd[2 * s + 1, 0:1, :], bnd[2 * s, 0:1, :])
            part = jnp.where(second, product[:, BLK:], product[:, :BLK])
            total += jnp.where(mark == own_col, part, 0.0)
        rows = pl.ds(pl.multiple_of(u * BLK, BLK), BLK)
        own = xv[rows, :]
        o_ref[rows, :] = (1.5 * own - 0.5 * total - 0.1 * total * total * total).astype(jnp.bfloat16)

    steps = (0, -2, 2, 4)

    def unit_at(r, i):
        return lax.rem(r + steps[i] + UNITS, UNITS)

    def multiply_sibling(i):
        for g in range(GROUPS):
            wait_for(sib.at[i, g], sb_r.at[i, g])
        multiply(sib, i, unit_at(sibling, i))

    multiply(pan, 0, unit_at(row, 0))
    for i in (1, 2, 3):
        for g in range(GROUPS):
            if i < 3:
                wait_for(pan.at[i, g], ag_r.at[i - 1, g])
            else:
                wait_for(pan.at[3, g, 0], ah_r.at[0, g])
                wait_for(pan.at[3, g, 1], ah_r.at[1, g])
            send(pan.at[i, g], sib.at[i, g], sb_s.at[i, g], sb_r.at[i, g], (sibling, col))
    multiply_sibling(0)
    for i in (1, 2, 3):
        multiply(pan, i, unit_at(row, i))
    for i in (1, 2, 3):
        multiply_sibling(i)
    for copy in sent:
        copy.wait_send()


def shards(n_row, block_values, block_cols, section_cols):
    blocks = n_row // 2 // STRIDE
    slots = CHUNKS + LANES * (blocks // 2 - 1)
    f32 = jnp.float32
    part = (2, PER, TILE, BLK)
    packet = (2, 2, TILE, BLK)
    held = (GROUPS, 2, 2, PER, TILE, BLK)
    band = (TILE + BLK, BLK)
    dma = pltpu.SemaphoreType.DMA
    return pl.pallas_call(
        functools.partial(broadcast_multiply, n_row),
        out_shape=jax.ShapeDtypeStruct(block_values.shape, jnp.bfloat16),
        in_specs=[
            pl.BlockSpec(memory_space=pltpu.SMEM),
            pl.BlockSpec(memory_space=pltpu.SMEM),
            pl.BlockSpec(memory_space=pl.ANY),
        ],
        out_specs=pl.BlockSpec(memory_space=pltpu.VMEM),
        scratch_shapes=[
            pltpu.VMEM(block_values.shape, f32),
            pltpu.VMEM((UNITS, GROUPS) + part, f32),
            pltpu.VMEM((5, GROUPS) + part, f32),
            pltpu.VMEM((4, GROUPS) + part[1:], f32),
            pltpu.VMEM((CHUNKS,) + packet, f32),
            pltpu.VMEM((2, CHUNKS) + packet, f32),
            pltpu.VMEM((2, slots) + packet, f32),
            pltpu.VMEM((4,) + held, f32),
            pltpu.VMEM((4,) + held, f32),
            pltpu.VMEM((4,) + band, f32),
            pltpu.VMEM((4,) + band, f32),
            pltpu.VMEM((4,) + band, f32),
            pltpu.VMEM((4,) + band, f32),
            pltpu.VMEM((2, 2 * BLK, 2 * BLK), jnp.bfloat16),
            pltpu.VMEM((2, BLK, 2 * BLK), jnp.bfloat16),
            dma,
            dma((5, GROUPS)), dma((5, GROUPS)),
            dma((4, GROUPS)), dma((4, GROUPS)),
            dma((2, slots)), dma((2, slots)),
            dma((2, GROUPS)), dma((2, GROUPS)),
            dma((2, GROUPS)), dma((2, GROUPS)),
            dma((4, GROUPS)), dma((4, GROUPS)),
            dma((3, SIDE - 1)), dma((3, SIDE)),
        ],
        compiler_params=pltpu.CompilerParams(
            collective_id=0, has_side_effects=True, vmem_limit_bytes=32 * 1024 * 1024
        ),
        cost_estimate=pl.CostEstimate(flops=400_000_000, bytes_accessed=800_000, transcendentals=0),
        name="broadcast_multiply",
    )(section_cols, block_cols, block_values)


def solution(mesh):
    return jax.shard_map(
        functools.partial(shards, mesh.shape["row"]),
        mesh=mesh,
        in_specs=(P("col", "row"), P("col", "row"), P()),
        out_specs=P("col", "row"),
        check_vma=False,
    )
```

```python
import functools

import jax
import jax.numpy as jnp
from jax import lax
from jax.experimental import pallas as pl
from jax.experimental.pallas import tpu as pltpu
from jax.sharding import PartitionSpec as P

MESH = pl.DeviceIdType.MESH
BLK = 128
TILE = 8
UNITS = 8
STRIDE = 4
GROUPS = 3
PER = 3
CHUNKS = GROUPS * PER
LANES = 4
SIDE = 4


def broadcast_multiply(
    n_row, sec_ref, cols_ref, xv, o_ref,
    xs, raw, rawh, cand, tx, rx, pan, sib, stage, bx, by, bnd, wh, wl,
    rs_s, rs_r, rh_s, rh_r, cv_s, cv_r, ag_s, ag_r, ah_s, ah_r, sb_s, sb_r, bs_s, bs_r,
):
    chips = n_row // 2
    blocks = chips // STRIDE
    far_hop = blocks // 2
    slots = CHUNKS + LANES * (far_hop - 1)
    whole = slots - LANES
    row = lax.axis_index("row")
    col = lax.axis_index("col")
    z, core = lax.div(row, 2), lax.rem(row, 2)
    cx, cy = lax.div(col, SIDE), lax.rem(col, SIDE)

    def at(dz, k):
        return lax.rem(z + dz + chips, chips) * 2 + k

    def unit(r):
        return lax.rem(r, UNITS)

    sibling = at(0, 1 - core)
    near = [at(dz, k) for dz in (-1, 1) for k in (0, 1)]
    far = [at(dz, k) for dz in (-2, 2) for k in (0, 1)]
    xs_peers = [lax.rem(cx + d, SIDE) for d in range(1, SIDE)]
    ys_peers = [lax.rem(cy + d, SIDE) for d in range(1, SIDE)]

    barrier = pltpu.get_barrier_semaphore()
    greet = [(r, col) for r in near + far + [sibling]]
    greet += [(row, px * SIDE + cy) for px in xs_peers]
    greet += [(row, cx * SIDE + py) for py in ys_peers]
    for device in greet:
        pl.semaphore_signal(barrier, inc=1, device_id=device, device_id_type=MESH)

    sent = []

    def send(src, dst, send_sem, recv_sem, device):
        copy = pltpu.make_async_remote_copy(
            src_ref=src, dst_ref=dst, send_sem=send_sem, recv_sem=recv_sem,
            device_id=device, device_id_type=MESH,
        )
        copy.start()
        sent.append(copy)
        return copy

    for u in range(UNITS):
        mark = jnp.full((TILE, BLK), cols_ref[u, 0].astype(jnp.float32), jnp.float32)
        for h in range(2):
            xs[u, 0, h, 0] = mark
            for k in range(1, CHUNKS):
                first = u * BLK + h * (BLK // 2) + (k - 1) * TILE
                xs[u, k // PER, h, k % PER] = xv[first : first + TILE, :]
    groups = [jnp.full((TILE, BLK), sec_ref[s], jnp.int32) for s in range(2)]
    for s in range(2):
        for q in range(2):
            for first in range(0, BLK + TILE, TILE):
                value = None
                for i in range(UNITS // 2):
                    u = 2 * i + q
                    if first == 0:
                        piece = jnp.full((TILE, BLK), cols_ref[u, 0].astype(jnp.float32), jnp.float32)
                    else:
                        start = u * BLK + first - TILE
                        piece = xv[start : start + TILE, :]
                    value = piece if i == 0 else jnp.where((groups[s] & 3) == i, piece, value)
                stage[2 * s + q, first : first + TILE] = value

    pl.semaphore_wait(barrier, len(greet))

    full_copies, half_copies = [], []
    for g in range(GROUPS):
        line = []
        for dz in (1, -1):
            for k in (0, 1):
                r = at(dz, k)
                slot = (1 if dz == 1 else 3) + core
                i = (0 if dz == 1 else 2) + k
                line.append(send(
                    xs.at[unit(r), g], raw.at[slot, g], rs_s.at[i, g], rs_r.at[slot, g], (r, col)
                ))
        line.append(send(
            xs.at[unit(sibling), g], raw.at[0, g], rs_s.at[4, g], rs_r.at[0, g], (sibling, col)
        ))
        full_copies.append(line)
        for dz in (2, -2):
            for k in (0, 1):
                r = at(dz, k)
                h = 0 if dz == 2 else 1
                slot = 2 * h + core
                i = 2 * h + k
                half_copies.append(send(
                    xs.at[unit(r), g, h], rawh.at[slot, g], rh_s.at[i, g], rh_r.at[slot, g], (r, col)
                ))

    def spread(src, dst, mine, peers, device, step):
        for d, p in enumerate(peers):
            send(src(p), dst.at[mine], bs_s.at[step, d], bs_r.at[step, mine], device(p))

    def arrived(dst, peers, step):
        for p in peers:
            pltpu.make_async_copy(dst.at[p], dst.at[p], bs_r.at[step, p]).wait()

    spread(lambda p: stage.at[p], bx, cx, xs_peers, lambda p: (row, p * SIDE + cy), 0)

    where_right = []
    for h in range(2):
        line = []
        for s in range(2):
            e = (z - (groups[s] >> 1)) & (chips - 1)
            m = e & (STRIDE - 1)
            v = jnp.where(m == 2, 2 if h == 0 else -2, jnp.where(m == 3, -1, m))
            line.append(((e - v) & (chips - 1)) >> 2)
        where_right.append(line)

    def wait_for(dst, sem):
        pltpu.make_async_copy(dst, dst, sem).wait()

    me_unit = unit(row)
    sources = [sibling] + near
    right4 = (at(STRIDE, core), col)
    left4 = (at(-STRIDE, core), col)

    def candidate(k):
        g, c = k // PER, k % PER
        for h in range(2):
            own = xs[me_unit, g, h, c]
            pieces = [(sources[i], raw[i, g, h, c]) for i in range(5)]
            pieces += [(far[2 * h + i], rawh[2 * h + i, g, c]) for i in range(2)]
            for s in range(2):
                value = own
                for r, piece in pieces:
                    value = jnp.where(groups[s] == r, piece, value)
                cand[k, h, s] = value
                pan[0, g, h, s, c] = value

    def consume(d, t):
        for hop in range(1, far_hop + 1):
            k = t - LANES * (hop - 1)
            if 0 <= k < CHUNKS:
                g, c = k // PER, k % PER
                place = hop if d == 0 else blocks - hop
                for h in range(2) if hop < far_hop else (d,):
                    for s in range(2):
                        pan[0, g, h, s, c] = jnp.where(
                            where_right[h][s] == place, rx[d, t, h, s], pan[0, g, h, s, c]
                        )

    def gather(g):
        send(pan.at[0, g], pan.at[1, g], ag_s.at[0, g], ag_r.at[0, g], (at(1, core), col))
        send(pan.at[0, g], pan.at[2, g], ag_s.at[1, g], ag_r.at[1, g], (at(-1, core), col))
        send(pan.at[0, g, 0], pan.at[3, g, 0], ah_s.at[0, g], ah_r.at[0, g], (at(2, core), col))
        send(pan.at[0, g, 1], pan.at[3, g, 1], ah_s.at[1, g], ah_r.at[1, g], (at(-2, core), col))
        send(pan.at[0, g], sib.at[0, g], sb_s.at[0, g], sb_r.at[0, g], (sibling, col))

    def pick(dst, into, mine, own, peers, place):
        for first in range(0, BLK + TILE, TILE):
            rows = pl.ds(first, TILE)
            value = own(rows)
            for p in peers:
                value = jnp.where(place == p, dst[p, rows], value)
            into[mine, rows] = value

    my_group = jnp.full((TILE, BLK), sec_ref[lax.div(cx, 2)], jnp.int32)

    def band_step_two():
        arrived(bx, xs_peers, 0)
        pick(bx, by, cy, lambda rows: stage[cx, rows], xs_peers, my_group >> 4)
        spread(lambda p: by.at[cy], by, cy, ys_peers, lambda p: (row, cx * SIDE + p), 1)

    def band_step_three():
        arrived(by, ys_peers, 1)
        pick(by, bnd, cx, lambda rows: by[cy, rows], ys_peers, (my_group >> 2) & 3)
        spread(lambda p: bnd.at[cx], bnd, cx, xs_peers, lambda p: (row, p * SIDE + cy), 2)

    def band_ready():
        arrived(bnd, xs_peers, 2)
        for s in range(2):
            for q in range(2):
                value = bnd[2 * s + q, TILE:]
                high = value.astype(jnp.bfloat16)
                low = (value - high.astype(jnp.float32)).astype(jnp.bfloat16)
                wh[s, :BLK, q * BLK : (q + 1) * BLK] = high
                wh[s, BLK:, q * BLK : (q + 1) * BLK] = high
                wl[s, :, q * BLK : (q + 1) * BLK] = low

    def packet(ref, d, t):
        return ref.at[d, t] if t < whole else ref.at[d, t, d]

    def received(d, t):
        wait_for(packet(rx, d, t), cv_r.at[d, t])

    def finish(t):
        k = t - LANES * (far_hop - 1)
        if k >= 0 and k % PER == PER - 1:
            gather(k // PER)

    for t in range(slots):
        if t < CHUNKS and t % PER == 0:
            g = t // PER
            for i in range(5):
                wait_for(raw.at[i, g], rs_r.at[i, g])
            for i in range(4):
                wait_for(rawh.at[i, g], rh_r.at[i, g])
            for k in range(t, t + PER):
                candidate(k)
        for d in range(2):
            target = right4 if d == 0 else left4
            if t >= LANES:
                received(d, t - LANES)
            if t < CHUNKS:
                for h in range(2):
                    for s in range(2):
                        value = cand[t, h, s]
                        if t >= LANES:
                            value = jnp.where(where_right[h][s] == 0, value, rx[d, t - LANES, h, s])
                        tx[d, t, h, s] = value
                source = tx.at[d, t]
            elif t < whole:
                source = rx.at[d, t - LANES]
            else:
                source = rx.at[d, t - LANES, d]
            send(source, packet(rx, d, t), cv_s.at[d, t], cv_r.at[d, t], target)
        if t >= LANES:
            for d in range(2):
                consume(d, t - LANES)
            finish(t - LANES)
        if t == LANES - 1:
            band_step_two()
        if t == 2 * LANES - 1:
            band_step_three()
        if t == 3 * LANES - 1:
            band_ready()
    for t in range(slots - LANES, slots):
        for d in range(2):
            received(d, t)
            consume(d, t)
        finish(t)

    def multiply(buf, i, u):
        total = jnp.zeros((BLK, BLK), jnp.float32)
        own_col = cols_ref[u, 0].astype(jnp.float32)
        for s in range(2):
            tiles = [
                buf[i, k // PER, h, s, k % PER] for h in range(2) for k in range(1, CHUNKS)
            ]
            value = jnp.concatenate(tiles, axis=0)
            high = value.astype(jnp.bfloat16)
            low = (value - high.astype(jnp.float32)).astype(jnp.bfloat16)
            both = jnp.concatenate([high, low], axis=1)
            product = jnp.dot(both, wh[s], preferred_element_type=jnp.float32)
            product += jnp.dot(high, wl[s], preferred_element_type=jnp.float32)
            second = buf[i, 0, 0, s, 0][0:1, :] > 0.5
            mark = jnp.where(second, bnd[2 * s + 1, 0:1, :], bnd[2 * s, 0:1, :])
            part = jnp.where(second, product[:, BLK:], product[:, :BLK])
            total += jnp.where(mark == own_col, part, 0.0)
        rows = pl.ds(pl.multiple_of(u * BLK, BLK), BLK)
        own = xv[rows, :]
        o_ref[rows, :] = (1.5 * own - 0.5 * total - 0.1 * total * total * total).astype(jnp.bfloat16)

    steps = (0, -2, 2, 4)

    def unit_at(r, i):
        return lax.rem(r + steps[i] + UNITS, UNITS)

    def multiply_sibling(i):
        for g in range(GROUPS):
            wait_for(sib.at[i, g], sb_r.at[i, g])
        multiply(sib, i, unit_at(sibling, i))

    multiply(pan, 0, unit_at(row, 0))
    for i in (1, 2, 3):
        for g in range(GROUPS):
            if i < 3:
                wait_for(pan.at[i, g], ag_r.at[i - 1, g])
            else:
                wait_for(pan.at[3, g, 0], ah_r.at[0, g])
                wait_for(pan.at[3, g, 1], ah_r.at[1, g])
            send(pan.at[i, g], sib.at[i, g], sb_s.at[i, g], sb_r.at[i, g], (sibling, col))
    multiply_sibling(0)
    for i in (1, 2, 3):
        multiply(pan, i, unit_at(row, i))
    for i in (1, 2, 3):
        multiply_sibling(i)
    for copy in sent:
        copy.wait_send()


def shards(n_row, block_values, block_cols, section_cols):
    blocks = n_row // 2 // STRIDE
    slots = CHUNKS + LANES * (blocks // 2 - 1)
    f32 = jnp.float32
    part = (2, PER, TILE, BLK)
    packet = (2, 2, TILE, BLK)
    held = (GROUPS, 2, 2, PER, TILE, BLK)
    band = (TILE + BLK, BLK)
    dma = pltpu.SemaphoreType.DMA
    return pl.pallas_call(
        functools.partial(broadcast_multiply, n_row),
        out_shape=jax.ShapeDtypeStruct(block_values.shape, jnp.bfloat16),
        in_specs=[
            pl.BlockSpec(memory_space=pltpu.SMEM),
            pl.BlockSpec(memory_space=pltpu.SMEM),
            pl.BlockSpec(memory_space=pltpu.VMEM),
        ],
        out_specs=pl.BlockSpec(memory_space=pltpu.VMEM),
        scratch_shapes=[
            pltpu.VMEM((UNITS, GROUPS) + part, f32),
            pltpu.VMEM((5, GROUPS) + part, f32),
            pltpu.VMEM((4, GROUPS) + part[1:], f32),
            pltpu.VMEM((CHUNKS,) + packet, f32),
            pltpu.VMEM((2, CHUNKS) + packet, f32),
            pltpu.VMEM((2, slots) + packet, f32),
            pltpu.VMEM((4,) + held, f32),
            pltpu.VMEM((4,) + held, f32),
            pltpu.VMEM((4,) + band, f32),
            pltpu.VMEM((4,) + band, f32),
            pltpu.VMEM((4,) + band, f32),
            pltpu.VMEM((4,) + band, f32),
            pltpu.VMEM((2, 2 * BLK, 2 * BLK), jnp.bfloat16),
            pltpu.VMEM((2, BLK, 2 * BLK), jnp.bfloat16),
            dma((5, GROUPS)), dma((5, GROUPS)),
            dma((4, GROUPS)), dma((4, GROUPS)),
            dma((2, slots)), dma((2, slots)),
            dma((2, GROUPS)), dma((2, GROUPS)),
            dma((2, GROUPS)), dma((2, GROUPS)),
            dma((4, GROUPS)), dma((4, GROUPS)),
            dma((3, SIDE - 1)), dma((3, SIDE)),
        ],
        compiler_params=pltpu.CompilerParams(
            collective_id=0, has_side_effects=True, vmem_limit_bytes=32 * 1024 * 1024
        ),
        cost_estimate=pl.CostEstimate(flops=400_000_000, bytes_accessed=800_000, transcendentals=0),
        name="broadcast_multiply",
    )(section_cols, block_cols, block_values)


def solution(mesh):
    return jax.shard_map(
        functools.partial(shards, mesh.shape["row"]),
        mesh=mesh,
        in_specs=(P("col", "row"), P("col", "row"), P()),
        out_specs=P("col", "row"),
        check_vma=False,
    )
```
